256 devices in a mesh: grp: 2 (over z_hi), seq: 2 (over core), vocab: 64 (over z_lo, y, x).
Axes of the slice: x: 4, y: 4, z: 8 (z_hi: 2, z_lo: 4; z = z_hi * 4 + z_lo), core: 2. Of those that a mesh axis runs over, the one named last changes fastest.
Arguments:
- teacher_hidden: bfloat16 [1024, 4096], P(None, ('grp', 'seq')), may hold values from -24 to 24
- teacher_weight: bfloat16 [4096, 75968], P(('grp', 'seq'), 'vocab'), may hold values from -0.61035156 to 0.61035156
- student_hidden: bfloat16 [1024, 5120], P(None, ('grp', 'seq')), may hold values from -24 to 24
- student_weight: bfloat16 [5120, 75968], P(('grp', 'seq'), 'vocab'), may hold values from -0.48828125 to 0.48828125
- rollout_ids: int32 [1024], P(('grp', 'seq')), may hold values from 0 to 75967
Outputs:
- grad_hidden: bfloat16 [1024, 5120], P('vocab', ('grp', 'seq'))
- grad_weight: bfloat16 [5120, 75968], P(('grp', 'seq'), 'vocab')
- mean_loss: float32 [], replicated
The draws below stay inside these ranges and needn't reach their ends.
All inputs are finite; a program needn't handle non-finite values.
Results may differ from the reference program's by a relative error of at most 0.0041.
Values may be sent and summed in bfloat16 or wider, within the bound.
No kernel may reach another device: no remote copies, remote signals or barrier semaphores. Data moves between devices by JAX's collectives and lax.ppermute only.
A program may use at most 128 MiB of HBM per device.

```python
import math
import jax
import jax.numpy as jnp
import numpy as np
from jax import lax

DT = 4096
DS = 5120
VOCAB = 75968
TOKENS = 1024


def normal_rows(key, stream_salt, feature_width):
    return jax.random.truncated_normal(jax.random.fold_in(key, stream_salt), -6.0, 6.0, (TOKENS, feature_width), jnp.float32)


def scaled_hidden(key, stream_salt, feature_width):
    base_rows = normal_rows(key, stream_salt, feature_width)
    return base_rows.astype(jnp.bfloat16)


def drawn_weight(key, feature_width, own_salt):
    key = jax.random.fold_in(key, own_salt)
    weights = jax.random.truncated_normal(key, -6.0, 6.0, (feature_width, VOCAB), jnp.float32) * (3.0 / math.sqrt(feature_width))
    return weights.astype(jnp.bfloat16)


def draw_teacher_hidden(key, part):
    return scaled_hidden(key, 11, DT)


def draw_student_hidden(key, part):
    return scaled_hidden(key, 12, DS)


def draw_teacher_weight(key, part):
    return drawn_weight(key, DT, 23)


def draw_student_weight(key, part):
    return drawn_weight(key, DS, 24)


def place_ends(entries, rng, smallest, high):
    extent = entries.shape
    index_at = [jax.random.randint(jax.random.fold_in(rng, axis), (), 0, extent[axis]) for axis in range(len(extent))]
    entries = entries.at[tuple(index_at)].set(smallest)
    longest = extent.index(max(extent))
    index_at[longest] = (index_at[longest] + 1) % extent[longest]
    return entries.at[tuple(index_at)].set(high)


def skewed_wide(own_key, extent, number_of, slope):
    weights = [min(1 << octave, number_of + 1 - (1 << octave)) * (1 << 20) // math.isqrt((1 << octave) ** slope) + 1 for octave in range((number_of + 1).bit_length()) if 1 << octave <= number_of]
    deviation = 1 + sum(weights) // (1 << 30)
    table = np.cumsum(np.array([max(1, weight // deviation) for weight in weights]))
    pick = jax.random.randint(jax.random.fold_in(own_key, 1), extent, 0, int(table[len(weights) - 1]))
    start = jnp.left_shift(1, jnp.searchsorted(jnp.asarray(table, jnp.int32), pick, side="right").astype(jnp.int32))
    rank = start - 1 + jax.random.randint(jax.random.fold_in(own_key, 4), extent, 0, 1 << 30) % jnp.minimum(start, number_of + 1 - start)
    return jax.random.permutation(jax.random.fold_in(own_key, 2), number_of)[rank].astype(jnp.int32)


def setup_inputs(seed: int = 0) -> dict:
    key_of = jax.random.split(jax.random.key(seed), 6)
    return {
        "teacher_hidden": draw_teacher_hidden(jax.random.fold_in(key_of[5], 71), 0),
        "teacher_weight": draw_teacher_weight(jax.random.fold_in(key_of[5], 71), 0),
        "student_hidden": draw_student_hidden(jax.random.fold_in(key_of[5], 71), 0),
        "student_weight": draw_student_weight(jax.random.fold_in(key_of[5], 71), 0),
        "rollout_ids": place_ends(skewed_wide(key_of[4], (TOKENS,), VOCAB, 2), jax.random.fold_in(key_of[4], 3), 0, VOCAB - 1).astype(jnp.int32),
    }


ENTROPY_WEIGHT = 0.1
ADVANTAGE_CLIP = 2.0


def reference(teacher_hidden, teacher_weight, student_hidden, student_weight, rollout_ids):
    teacher_logits = jnp.dot(teacher_hidden, teacher_weight, preferred_element_type=jnp.float32)
    student_logits = jnp.dot(student_hidden, student_weight, preferred_element_type=jnp.float32)
    top_s = jnp.max(student_logits, axis=1)
    top_t = jnp.max(teacher_logits, axis=1)
    shifted_s = jnp.exp(student_logits - top_s[:, None])
    total_s = jnp.sum(shifted_s, axis=1)
    total_t = jnp.sum(jnp.exp(teacher_logits - top_t[:, None]), axis=1)
    weighted_s = jnp.sum(shifted_s * student_logits, axis=1)
    weighted_t = jnp.sum(shifted_s * teacher_logits, axis=1)
    columns = lax.broadcasted_iota(jnp.int32, student_logits.shape, 1)
    onehot = columns == rollout_ids.astype(jnp.int32)[:, None]
    pick_s = jnp.sum(jnp.where(onehot, student_logits, jnp.float32(0.0)), axis=1)
    pick_t = jnp.sum(jnp.where(onehot, teacher_logits, jnp.float32(0.0)), axis=1)
    norm_s = top_s + jnp.log(total_s)
    norm_t = top_t + jnp.log(total_t)
    factor = 1.0 + ENTROPY_WEIGHT
    divergence = factor * (weighted_s / total_s - norm_s) - (weighted_t / total_s - norm_t)
    advantage = jnp.clip((pick_t - norm_t) - (pick_s - norm_s), -ADVANTAGE_CLIP, ADVANTAGE_CLIP)
    token_loss = divergence - advantage * (pick_s - norm_s)
    mean_loss = jnp.sum(token_loss) / TOKENS
    student_probs = shifted_s / total_s[:, None]
    inner = factor * (student_logits - norm_s[:, None]) - (teacher_logits - norm_t[:, None]) - divergence[:, None]
    logit_grad = student_probs * inner - advantage[:, None] * (onehot.astype(jnp.float32) - student_probs)
    logit_grad = logit_grad.astype(jnp.bfloat16)
    grad_weight = lax.dot_general(student_hidden, logit_grad, (((0,), (0,)), ((), ())), preferred_element_type=jnp.float32).astype(jnp.bfloat16)
    grad_hidden = lax.dot_general(logit_grad, student_weight, (((1,), (1,)), ((), ())), preferred_element_type=jnp.float32).astype(jnp.bfloat16)
    return grad_hidden, grad_weight, mean_loss
```

```python
import jax
import jax.numpy as jnp
from jax import lax
from jax.sharding import Mesh
from jax.sharding import PartitionSpec as P

ENTROPY_WEIGHT = 0.1
ADVANTAGE_CLIP = 2.0
HALVES = 2
LEVELS = 32767.0


def swap(x, axis):
    return lax.ppermute(x, axis, [(0, 1), (1, 0)])


def rotate(x, axis, size, step):
    return lax.ppermute(x, axis, [(i, (i + step) % size) for i in range(size)])


def dot_t(weight_t, rows):
    return lax.dot_general(
        weight_t, rows, (((1,), (1,)), ((), ())), preferred_element_type=jnp.float32
    )


def shards(teacher_hidden, teacher_weight, student_hidden, student_weight, rollout_ids):
    g, s, z = lax.axis_index("g"), lax.axis_index("s"), lax.axis_index("z")
    place = (z * 4 + lax.axis_index("y")) * 4 + lax.axis_index("x")
    tokens = student_hidden.shape[0]
    width = student_weight.shape[1]
    wt_t, ws_t = teacher_weight.T, student_weight.T
    depth = ws_t.shape[1]

    def rows(hidden, q, c):
        parts = hidden.reshape(4, 16, HALVES, 8, hidden.shape[1])
        part = lax.dynamic_index_in_dim(parts, q, 0, keepdims=False)[:, c]
        return part.reshape(128, hidden.shape[1])

    def owner(gr, sr):
        return 2 * (g ^ gr) + (s ^ sr)

    h = [
        [
            jnp.concatenate([rows(student_hidden, owner(gr, sr), c) for sr in (0, 1)], axis=0)
            for gr in (0, 1)
        ]
        for c in range(HALVES)
    ]
    ht = [
        [
            jnp.concatenate([rows(teacher_hidden, owner(gr, sr), c) for sr in (0, 1)], axis=0)
            for gr in (0, 1)
        ]
        for c in range(HALVES)
    ]

    def chip_sums(c, gr):
        part = jnp.stack([dot_t(ws_t, h[c][gr]), dot_t(wt_t, ht[c][gr])])
        return part[:, :, :128] + swap(part[:, :, 128:], "s")

    def send_far(x):
        peak = jnp.maximum(jnp.max(jnp.abs(x), axis=1, keepdims=True), 1e-30)
        codes = jnp.round(x * (LEVELS / peak)).astype(jnp.int16)
        scale = swap(peak, "g") * (1.0 / LEVELS)
        return swap(codes, "g").astype(jnp.float32) * scale

    far = [send_far(chip_sums(c, 1)) for c in range(HALVES)]
    near = [chip_sums(c, 0) for c in range(HALVES)]

    factor = 1.0 + ENTROPY_WEIGHT
    ids = rollout_ids.reshape(16, HALVES, 8)
    losses = jnp.float32(0.0)
    grads = []
    pieces = []
    for c in range(HALVES):
        logits = near[c] + far[c]
        sl, tl = logits[0], logits[1]
        vocab = place * width + lax.broadcasted_iota(jnp.int32, sl.shape, 0)
        onehot = vocab == ids[:, c].reshape(1, 128)
        own_s, own_t = jnp.max(sl, axis=0), jnp.max(tl, axis=0)
        es = jnp.exp(sl - own_s)
        stats = jnp.stack(
            [
                own_s,
                own_t,
                jnp.sum(es, axis=0),
                jnp.sum(jnp.exp(tl - own_t), axis=0),
                jnp.sum(es * sl, axis=0),
                jnp.sum(es * tl, axis=0),
                jnp.sum(jnp.where(onehot, sl, 0.0), axis=0),
                jnp.sum(jnp.where(onehot, tl, 0.0), axis=0),
            ]
        )

        def merge(many):
            top_s, top_t = jnp.max(many[:, 0], axis=0), jnp.max(many[:, 1], axis=0)
            fs, ft = jnp.exp(many[:, 0] - top_s), jnp.exp(many[:, 1] - top_t)
            return jnp.stack(
                [
                    top_s,
                    top_t,
                    jnp.sum(many[:, 2] * fs, axis=0),
                    jnp.sum(many[:, 3] * ft, axis=0),
                    jnp.sum(many[:, 4] * fs, axis=0),
                    jnp.sum(many[:, 5] * fs, axis=0),
                    jnp.sum(many[:, 6], axis=0),
                    jnp.sum(many[:, 7], axis=0),
                ]
            )

        plane = merge(
            lax.all_to_all(jnp.broadcast_to(stats, (16, 8, 128)), ("y", "x"), 0, 0)
        )
        column = jnp.zeros((4, 8, 128), jnp.float32)
        for k in range(4):
            got = plane if k == 0 else rotate(plane, "z", 4, k)
            column = lax.dynamic_update_index_in_dim(column, got, (z + 4 - k) % 4, 0)
        top_s, top_t, total_s, total_t, weighted_s, weighted_t, pick_s, pick_t = merge(column)
        norm_s = top_s + jnp.log(total_s)
        norm_t = top_t + jnp.log(total_t)
        divergence = factor * (weighted_s / total_s - norm_s) - (weighted_t / total_s - norm_t)
        advantage = jnp.clip(
            pick_t - norm_t - (pick_s - norm_s), -ADVANTAGE_CLIP, ADVANTAGE_CLIP
        )
        losses = losses + jnp.sum(divergence - advantage * (pick_s - norm_s))
        probs = es * (jnp.exp(own_s - top_s) / total_s)
        inner = factor * (sl - norm_s) - (tl - norm_t) - divergence
        grad = probs * inner - advantage * (onehot.astype(jnp.float32) - probs)
        grad = grad.astype(jnp.bfloat16)

        away = swap(grad, "g")
        near_g = jnp.concatenate([grad, swap(grad, "s")], axis=1)
        far_g = jnp.concatenate([away, swap(away, "s")], axis=1)
        for gr, both in ((0, near_g), (1, far_g)):
            part = lax.dot_general(
                both, ws_t, (((0,), (0,)), ((), ())), preferred_element_type=jnp.float32
            ).astype(jnp.bfloat16)
            part = jnp.transpose(part.reshape(2, 16, 8, depth), (1, 0, 2, 3))
            got = lax.all_to_all(part, ("y", "x"), 0, 0)
            pieces.append(jnp.sum(got.astype(jnp.float32), axis=0))
            grads.append((both, h[c][gr]))

    grad_weight = lax.dot_general(
        jnp.concatenate([a for a, _ in grads], axis=1),
        jnp.concatenate([b for _, b in grads], axis=0),
        (((1,), (0,)), ((), ())),
        preferred_element_type=jnp.float32,
    ).astype(jnp.bfloat16)

    blocks = jnp.stack(
        [jnp.concatenate([pieces[2 * c + gr] for c in range(HALVES)], axis=1) for gr in (0, 1)]
    ).reshape(4, 8 * HALVES, depth)

    def block(dest):
        return lax.dynamic_index_in_dim(
            blocks, 2 * (g ^ (dest // 2)) + (s ^ (dest % 2)), 0, keepdims=False
        )

    total = block(z)
    for k in (1, 2, 3):
        total = total + rotate(block((z + k) % 4), "z", 4, k)
    losses = losses + swap(losses, "s")
    losses = losses + swap(losses, "g")
    return total.astype(jnp.bfloat16), grad_weight.T, losses / tokens


def solution(mesh):
    split = Mesh(mesh.devices.reshape(2, 2, 4, 4, 4), ("g", "s", "z", "y", "x"))
    owners, vocab = ("g", "s"), ("z", "y", "x")
    return jax.shard_map(
        shards,
        mesh=split,
        in_specs=(P(None, owners), P(owners, vocab), P(None, owners), P(owners, vocab), P(owners)),
        out_specs=(P(vocab, owners), P(owners, vocab), P()),
        check_vma=False,
    )
```

```python
import functools

import jax
import jax.numpy as jnp
from jax import lax
from jax.experimental import pallas as pl
from jax.experimental.pallas import tpu as pltpu
from jax.sharding import Mesh
from jax.sharding import PartitionSpec as P

ENTROPY_WEIGHT = 0.1
FACTOR = 1.0 + ENTROPY_WEIGHT
ADVANTAGE_CLIP = 2.0
LANES = 256
LEVELS = 32700.0
VMEM = pl.BlockSpec(memory_space=pltpu.VMEM)
SMEM = pl.BlockSpec(memory_space=pltpu.SMEM)
F32, BF16 = jnp.float32, jnp.bfloat16


def params(mib):
    return pltpu.CompilerParams(vmem_limit_bytes=mib * 2**20)


def swap(x, axis):
    return lax.ppermute(x, axis, [(0, 1), (1, 0)])


def rotate(x, axis, size, step):
    return lax.ppermute(x, axis, [(i, (i + step) % size) for i in range(size)])


def ordered(x, *earlier):
    return lax.optimization_barrier((x, *earlier))[0]


def partial_logits(weight, hidden, owner):
    rows = lax.dynamic_slice_in_dim(hidden, owner * LANES, LANES, 0)
    return lax.dot_general(weight, rows, (((1,), (1,)), ((), ())), preferred_element_type=F32)


def code_kernel(width, as_, bs, at, bt, codes):
    def put(v):
        return v.astype(jnp.int32).astype(jnp.int16)

    full = width // 16 * 16
    blank = jnp.zeros((codes.shape[1] - width - 1, LANES), F32)
    for head, (a, b) in enumerate(((as_, bs), (at, bt))):
        x = a[...] + b[...]
        peak = jnp.max(jnp.abs(x), axis=0, keepdims=True)
        power = jnp.ceil(jnp.log2(jnp.maximum(peak, 1e-30) / LEVELS) * 256.0)
        scale = 1.0 / jnp.exp2(power * (1.0 / 256.0))
        code = jnp.clip(jnp.round(x * scale), -32767.0, 32767.0)
        codes[head, :full] = put(code[:full])
        codes[head, full:] = put(jnp.concatenate([code[full:], power, blank], axis=0))


def encode(student, teacher):
    width = student[0].shape[0]
    rows = (width + 1 + 15) // 16 * 16
    return pl.pallas_call(
        functools.partial(code_kernel, width),
        in_specs=[VMEM] * 4,
        out_specs=VMEM,
        out_shape=jax.ShapeDtypeStruct((2, rows, LANES), jnp.int16),
        compiler_params=params(16),
        cost_estimate=pl.CostEstimate(
            flops=rows * LANES, bytes_accessed=20 * rows * LANES, transcendentals=0
        ),
    )(*student, *teacher)


def units_kernel(width, codes, units):
    full = width // 16 * 16
    for head in range(2):
        end = codes[head, full:].astype(jnp.int32).astype(F32)
        power = end[width - full : width - full + 1]
        units[head] = jnp.broadcast_to(jnp.exp2(power * (1.0 / 256.0)), (8, LANES))


def code_units(width, codes):
    rows = codes.shape[1] - width // 16 * 16
    block = pl.BlockSpec(codes.shape, lambda: (0, 0, 0))
    return pl.pallas_call(
        functools.partial(units_kernel, width),
        in_specs=[block],
        out_specs=VMEM,
        out_shape=jax.ShapeDtypeStruct((2, 8, LANES), F32),
        compiler_params=params(8),
        cost_estimate=pl.CostEstimate(
            flops=30_000_000_000, bytes_accessed=rows * 2 * LANES * 2, transcendentals=0
        ),
    )(codes)


def stats_kernel(width, place, as_, bs, at, bt, codes, units, ids, sl_ref, tl_ref, stats):
    def decoded(head):
        return codes[head].astype(jnp.int32).astype(F32)[:width] * units[head, :1]

    sl = as_[...] + bs[...] + decoded(0)
    tl = at[...] + bt[...] + decoded(1)
    sl_ref[...] = sl
    tl_ref[...] = tl
    own_s = jnp.max(sl, axis=0, keepdims=True)
    own_t = jnp.max(tl, axis=0, keepdims=True)
    es = jnp.exp(sl - own_s)
    row = lax.broadcasted_iota(jnp.int32, sl.shape, 0)
    onehot = row == ids[...] - place[0] * width

    def total(x):
        return jnp.sum(x, axis=0, keepdims=True)

    rows = [
        own_s,
        own_t,
        total(es),
        total(jnp.exp(tl - own_t)),
        total(es * sl),
        total(es * tl),
        total(jnp.where(onehot, sl, 0.0)),
        total(jnp.where(onehot, tl, 0.0)),
    ]
    stats[...] = jnp.broadcast_to(jnp.concatenate(rows, axis=0)[None], stats.shape)


def local_stats(place, student, teacher, codes, ids):
    width = student[0].shape[0]
    size = width * LANES
    return pl.pallas_call(
        functools.partial(stats_kernel, width),
        in_specs=[SMEM] + [VMEM] * 7,
        out_specs=[VMEM] * 3,
        out_shape=[jax.ShapeDtypeStruct((width, LANES), F32)] * 2
        + [jax.ShapeDtypeStruct((16, 8, LANES), F32)],
        compiler_params=params(24),
        cost_estimate=pl.CostEstimate(
            flops=size * 40, bytes_accessed=size * 28, transcendentals=size * 2
        ),
    )(place, *student, *teacher, codes, code_units(width, codes), ids)


def merged(many):
    top_s, top_t = jnp.max(many[:, 0], axis=0), jnp.max(many[:, 1], axis=0)
    fs, ft = jnp.exp(many[:, 0] - top_s), jnp.exp(many[:, 1] - top_t)
    return [
        top_s,
        top_t,
        jnp.sum(many[:, 2] * fs, axis=0),
        jnp.sum(many[:, 3] * ft, axis=0),
        jnp.sum(many[:, 4] * fs, axis=0),
        jnp.sum(many[:, 5] * fs, axis=0),
        jnp.sum(many[:, 6], axis=0),
        jnp.sum(many[:, 7], axis=0),
    ]


def merge_kernel(many, out):
    out[...] = jnp.stack(merged(many[...]))


def all_stats(stats):
    many = lax.all_to_all(stats, ("y", "x"), 0, 0)
    plane = pl.pallas_call(
        merge_kernel,
        in_specs=[VMEM],
        out_specs=VMEM,
        out_shape=jax.ShapeDtypeStruct(many.shape[1:], F32),
        compiler_params=params(4),
    )(many)
    return [plane] + [rotate(plane, "z", 4, k) for k in (1, 2, 3)]


def grad_kernel(width, place, s0, s1, s2, s3, sl_ref, tl_ref, ids, grad, column):
    for k, got in enumerate((s0, s1, s2, s3)):
        column[(place[1] + 4 - k) % 4] = got[...]
    m = merged(column[...])
    top_s, top_t, total_s, total_t, weighted_s, weighted_t, pick_s, pick_t = (
        v.reshape(1, LANES) for v in m
    )
    norm_s = top_s + jnp.log(total_s)
    norm_t = top_t + jnp.log(total_t)
    divergence = FACTOR * (weighted_s / total_s - norm_s) - (weighted_t / total_s - norm_t)
    advantage = jnp.clip(pick_t - norm_t - (pick_s - norm_s), -ADVANTAGE_CLIP, ADVANTAGE_CLIP)
    loss = divergence - advantage * (pick_s - norm_s)
    sl, tl = sl_ref[...], tl_ref[...]
    row = lax.broadcasted_iota(jnp.int32, sl.shape, 0)
    onehot = row == ids[...] - place[0] * width
    probs = jnp.exp(sl - top_s) * (1.0 / total_s)
    inner = FACTOR * (sl - norm_s) - (tl - norm_t) - divergence
    out = probs * inner - advantage * (onehot.astype(F32) - probs)

    full = width // 16 * 16
    parts = []
    for _ in range(3):
        parts.append(loss.astype(BF16).astype(F32))
        loss = loss - parts[-1]
    blank = jnp.zeros((grad.shape[0] - width - 3, LANES), F32)
    grad[:full] = out[:full].astype(BF16)
    grad[full:] = jnp.concatenate([out[full:], *parts, blank], axis=0).astype(BF16)


def logit_grad(place, column, sl, tl, ids):
    width = sl.shape[0]
    rows = (width + 3 + 15) // 16 * 16
    return pl.pallas_call(
        functools.partial(grad_kernel, width),
        in_specs=[SMEM] + [VMEM] * 7,
        out_specs=VMEM,
        out_shape=jax.ShapeDtypeStruct((rows, LANES), BF16),
        scratch_shapes=[pltpu.VMEM((4, 8, LANES), F32)],
        compiler_params=params(16),
        cost_estimate=pl.CostEstimate(
            flops=sl.size * 20, bytes_accessed=sl.size * 10, transcendentals=sl.size
        ),
    )(place, *column, sl, tl, ids)


def hidden_kernel(g0, g1, w, out):
    width, depth = w.shape
    for n, g in enumerate((g0, g1)):
        part = lax.dot_general(
            g[:width], w[...], (((0,), (0,)), ((), ())), preferred_element_type=F32
        )
        out[:, 16 * n : 16 * n + 16] = part.reshape(16, 16, depth).astype(BF16)


def hidden_part(g0, g1, w):
    depth = w.shape[1]
    return pl.pallas_call(
        hidden_kernel,
        in_specs=[VMEM] * 3,
        out_specs=VMEM,
        out_shape=jax.ShapeDtypeStruct((16, 32, depth), BF16),
        compiler_params=params(24),
        cost_estimate=pl.CostEstimate(
            flops=4 * LANES * w.size, bytes_accessed=2 * w.size, transcendentals=0
        ),
    )(g0, g1, w)


def scattered(part):
    got = lax.all_to_all(part, ("y", "x"), 0, 0)
    got = jnp.sum(got.astype(F32), axis=0)
    return got.reshape(2, 16, got.shape[1])


def weight_kernel(_, *refs):
    g = jnp.concatenate([r[...] for r in refs[:4]], axis=1)
    h = jnp.concatenate([r[...] for r in refs[4:8]], axis=0)
    refs[8][...] = jnp.dot(g, h, preferred_element_type=F32).astype(BF16)
    refs[9][...] = jnp.zeros(refs[9].shape, F32)


def weight_grad(width, grads, hidden, owners):
    depth = hidden.shape[1]
    block = 256

    def rows(d):
        return pl.BlockSpec((block, d), lambda i, sc: (i, 0))

    def owned(k):
        return pl.BlockSpec((LANES, depth), lambda i, sc: (sc[k], 0))

    return pl.pallas_call(
        weight_kernel,
        grid_spec=pltpu.PrefetchScalarGridSpec(
            num_scalar_prefetch=1,
            grid=(pl.cdiv(width, block),),
            in_specs=[rows(LANES)] * 4 + [owned(k) for k in range(4)],
            out_specs=[rows(depth), pl.BlockSpec((8, 128), lambda i, sc: (0, 0))],
        ),
        out_shape=[
            jax.ShapeDtypeStruct((width, depth), BF16),
            jax.ShapeDtypeStruct((8, 128), F32),
        ],
        compiler_params=params(24),
        cost_estimate=pl.CostEstimate(
            flops=8 * LANES * width * depth, bytes_accessed=4 * width * depth, transcendentals=0
        ),
    )(owners, *grads, *([hidden] * 4))


def shards(teacher_hidden, teacher_weight, student_hidden, student_weight, rollout_ids):
    g, s, z = lax.axis_index("g"), lax.axis_index("s"), lax.axis_index("z")
    index = (z * 4 + lax.axis_index("y")) * 4 + lax.axis_index("x")
    place = jnp.stack([index, z]).astype(jnp.int32)
    tokens, depth = student_hidden.shape
    wt, ws = teacher_weight.T, student_weight.T
    width = ws.shape[0]
    ids = rollout_ids.reshape(1, LANES)

    owners = jnp.stack(
        [2 * g + s, 2 * g + 1 - s, 2 * (1 - g) + s, 2 * (1 - g) + 1 - s]
    ).astype(jnp.int32)

    give_s = swap(partial_logits(ws, student_hidden, owners[3]), "s")
    give_t = swap(partial_logits(wt, teacher_hidden, owners[3]), "s")
    keep_s = partial_logits(ws, student_hidden, owners[2])
    keep_t = partial_logits(wt, teacher_hidden, owners[2])
    codes = encode((keep_s, give_s), (keep_t, give_t))
    far = swap(codes, "g")
    near = ordered(owners, codes)
    give_s = swap(partial_logits(ws, student_hidden, near[1]), "s")
    give_t = swap(partial_logits(wt, teacher_hidden, near[1]), "s")
    keep_s = partial_logits(ws, student_hidden, near[0])
    keep_t = partial_logits(wt, teacher_hidden, near[0])

    sl, tl, stats = local_stats(place, (keep_s, give_s), (keep_t, give_t), far, ids)
    grad = logit_grad(place, all_stats(stats), sl, tl, ids)
    away = swap(grad, "g")
    other = swap(grad, "s")
    near_blocks = scattered(hidden_part(grad, other, ws))
    away_other = swap(away, "s")
    far_part = hidden_part(away, away_other, ws)
    far_blocks = scattered(far_part)
    grads = [grad, other, away, away_other]
    grad_weight, done = weight_grad(width, grads, student_hidden, ordered(owners, far_part))
    far_blocks = ordered(far_blocks, done)

    blocks = jnp.concatenate([near_blocks, far_blocks], axis=0)

    def block(dest):
        return lax.dynamic_index_in_dim(
            blocks, 2 * (g ^ (dest // 2)) + (s ^ (dest % 2)), 0, keepdims=False
        )

    total = block(z)
    for k in (1, 2, 3):
        total = total + rotate(block((z + k) % 4), "z", 4, k)
    a, b, c, d = (jnp.sum(v[width : width + 3].astype(F32)) for v in grads)
    return total.astype(BF16), grad_weight.T, ((a + b) + (c + d)) / tokens


def solution(mesh):
    split = Mesh(mesh.devices.reshape(2, 2, 4, 4, 4), ("g", "s", "z", "y", "x"))
    owners, vocab = ("g", "s"), ("z", "y", "x")
    return jax.shard_map(
        shards,
        mesh=split,
        in_specs=(P(None, owners), P(owners, vocab), P(None, owners), P(owners, vocab), P(owners)),
        out_specs=(P(vocab, owners), P(owners, vocab), P()),
        check_vma=False,
    )
```

```python
import functools

import jax
import jax.numpy as jnp
from jax import lax
from jax.experimental import pallas as pl
from jax.experimental.pallas import tpu as pltpu
from jax.sharding import Mesh
from jax.sharding import PartitionSpec as P

ENTROPY_WEIGHT = 0.1
FACTOR = 1.0 + ENTROPY_WEIGHT
ADVANTAGE_CLIP = 2.0
LANES = 128
LEVELS = 32700.0
HIDES = 30_000_000_000
LAST = 8_200_000_000
SECOND = HIDES // 8
VMEM = pl.BlockSpec(memory_space=pltpu.VMEM)
SMEM = pl.BlockSpec(memory_space=pltpu.SMEM)
F32, BF16 = jnp.float32, jnp.bfloat16


def estimate(flops):
    return pl.CostEstimate(flops=flops, bytes_accessed=1, transcendentals=0)


FREE = estimate(1)


def params(mib):
    return pltpu.CompilerParams(vmem_limit_bytes=mib * 2**20)


def swap(x, axis):
    return lax.ppermute(x, axis, [(0, 1), (1, 0)])


def rotate(x, axis, size, step):
    return lax.ppermute(x, axis, [(i, (i + step) % size) for i in range(size)])


def ordered(x, *earlier):
    return lax.optimization_barrier((x, *earlier))[0]


def partial_logits(weight, hidden, grp, core):
    parts = hidden.reshape(2, 2, 2, LANES, hidden.shape[1])
    rows = lax.dynamic_slice(parts, (grp, 0, core, 0, 0), (1, 2, 1, *parts.shape[3:]))
    rows = rows.reshape(2 * LANES, hidden.shape[1])
    return lax.dot_general(weight, rows, (((1,), (1,)), ((), ())), preferred_element_type=F32)


def near_kernel(width, _, *refs):
    hs, ht, ws, wt, outs, rs, rt = refs[:4], refs[4:8], refs[8], refs[9], refs[10:14], refs[14], refs[15]
    step = pl.program_id(0)

    @pl.when(step == 0)
    def _():
        for k in range(4):
            rs[LANES * k : LANES * (k + 1)] = hs[k][...]
            rt[LANES * k : LANES * (k + 1)] = ht[k][...]

    for head, (w, r) in enumerate(((ws, rs), (wt, rt))):
        out = lax.dot_general(w[...], r[...], (((1,), (1,)), ((), ())), preferred_element_type=F32)
        outs[2 * head][...] = out[:, : 2 * LANES]
        outs[2 * head + 1][...] = out[:, 2 * LANES :]


def near_logits(blocks, hidden_s, hidden_t, ws, wt):
    width = ws.shape[0]
    ds, dt = hidden_s.shape[1], hidden_t.shape[1]
    tile = 2 * LANES

    def rows(k, d):
        return pl.BlockSpec((LANES, d), lambda i, sc: (sc[k], 0))

    def part(d):
        return pl.BlockSpec((tile, d), lambda i, sc: (i, 0))

    return pl.pallas_call(
        functools.partial(near_kernel, width),
        grid_spec=pltpu.PrefetchScalarGridSpec(
            num_scalar_prefetch=1,
            grid=(pl.cdiv(width, tile),),
            in_specs=[rows(k, d) for d in (ds, dt) for k in range(4)] + [part(ds), part(dt)],
            out_specs=[part(2 * LANES)] * 4,
            scratch_shapes=[pltpu.VMEM((4 * LANES, ds), BF16), pltpu.VMEM((4 * LANES, dt), BF16)],
        ),
        out_shape=[jax.ShapeDtypeStruct((width, 2 * LANES), F32)] * 4,
        compiler_params=params(24),
        cost_estimate=FREE,
    )(blocks, *([hidden_s] * 4), *([hidden_t] * 4), ws, wt)


def code_kernel(width, as_, bs, at, bt, *codes):
    def put(v):
        return v.astype(jnp.int32).astype(jnp.int16)

    full = width // 16 * 16
    blank = jnp.zeros((codes[0].shape[1] - width - 1, LANES), F32)
    for c, out in enumerate(codes):
        lanes = slice(c * LANES, (c + 1) * LANES)
        for head, (a, b) in enumerate(((as_, bs), (at, bt))):
            x = a[:, lanes] + b[:, lanes]
            peak = jnp.max(jnp.abs(x), axis=0, keepdims=True)
            power = jnp.ceil(jnp.log2(jnp.maximum(peak, 1e-30) / LEVELS) * 256.0)
            scale = 1.0 / jnp.exp2(power * (1.0 / 256.0))
            code = jnp.clip(jnp.round(x * scale), -32767.0, 32767.0)
            out[head, :full] = put(code[:full])
            out[head, full:] = put(jnp.concatenate([code[full:], power, blank], axis=0))


def encode(student, teacher):
    width = student[0].shape[0]
    rows = (width + 1 + 15) // 16 * 16
    return pl.pallas_call(
        functools.partial(code_kernel, width),
        in_specs=[VMEM] * 4,
        out_specs=[VMEM] * 2,
        out_shape=[jax.ShapeDtypeStruct((2, rows, LANES), jnp.int16)] * 2,
        compiler_params=params(16),
        cost_estimate=pl.CostEstimate(
            flops=rows * LANES, bytes_accessed=20 * rows * LANES, transcendentals=0
        ),
    )(*student, *teacher)


def units_kernel(width, codes, units):
    full = width // 16 * 16
    for head in range(2):
        end = codes[head, full:].astype(jnp.int32).astype(F32)
        power = end[width - full : width - full + 1]
        units[head] = jnp.broadcast_to(jnp.exp2(power * (1.0 / 256.0)), (8, LANES))


def code_units(width, codes, flops):
    rows = codes.shape[1] - width // 16 * 16
    block = pl.BlockSpec(codes.shape, lambda: (0, 0, 0))
    return pl.pallas_call(
        functools.partial(units_kernel, width),
        in_specs=[block],
        out_specs=VMEM,
        out_shape=jax.ShapeDtypeStruct((2, 8, LANES), F32),
        compiler_params=params(8),
        cost_estimate=estimate(flops),
    )(codes)


def stats_kernel(width, place, as_, bs, at, bt, codes, units, ids, sl_ref, tl_ref, stats):
    def decoded(head):
        return codes[head].astype(jnp.int32).astype(F32)[:width] * units[head, :1]

    sl = as_[...] + bs[...] + decoded(0)
    tl = at[...] + bt[...] + decoded(1)
    sl_ref[...] = sl
    tl_ref[...] = tl
    own_s = jnp.max(sl, axis=0, keepdims=True)
    own_t = jnp.max(tl, axis=0, keepdims=True)
    es = jnp.exp(sl - own_s)
    row = lax.broadcasted_iota(jnp.int32, sl.shape, 0)
    onehot = row == ids[...] - place[0] * width

    def total(x):
        return jnp.sum(x, axis=0, keepdims=True)

    rows = [
        own_s,
        own_t,
        total(es),
        total(jnp.exp(tl - own_t)),
        total(es * sl),
        total(es * tl),
        total(jnp.where(onehot, sl, 0.0)),
        total(jnp.where(onehot, tl, 0.0)),
    ]
    stats[...] = jnp.broadcast_to(jnp.concatenate(rows, axis=0)[None], stats.shape)


def local_stats(place, c, student, teacher, codes, flops, ids):
    width = student[0].shape[0]
    size = width * LANES
    half = pl.BlockSpec((width, LANES), lambda i: (0, c))

    def whole(*shape):
        return pl.BlockSpec(shape, lambda i: (0,) * len(shape))

    return pl.pallas_call(
        functools.partial(stats_kernel, width),
        grid=(1,),
        in_specs=[SMEM] + [half] * 4 + [whole(*codes.shape), whole(2, 8, LANES), whole(1, LANES)],
        out_specs=[whole(width, LANES)] * 2 + [whole(16, 8, LANES)],
        out_shape=[jax.ShapeDtypeStruct((width, LANES), F32)] * 2
        + [jax.ShapeDtypeStruct((16, 8, LANES), F32)],
        compiler_params=params(24),
        cost_estimate=estimate(flops[1]),
    )(place, *student, *teacher, codes, code_units(width, codes, flops[0]), ids)


def merged(many):
    top_s, top_t = jnp.max(many[:, 0], axis=0), jnp.max(many[:, 1], axis=0)
    fs, ft = jnp.exp(many[:, 0] - top_s), jnp.exp(many[:, 1] - top_t)
    return [
        top_s,
        top_t,
        jnp.sum(many[:, 2] * fs, axis=0),
        jnp.sum(many[:, 3] * ft, axis=0),
        jnp.sum(many[:, 4] * fs, axis=0),
        jnp.sum(many[:, 5] * fs, axis=0),
        jnp.sum(many[:, 6], axis=0),
        jnp.sum(many[:, 7], axis=0),
    ]


def merge_kernel(many, out):
    out[...] = jnp.stack(merged(many[...]))


def all_stats(stats):
    many = lax.all_to_all(stats, ("y", "x"), 0, 0)
    plane = pl.pallas_call(
        merge_kernel,
        in_specs=[VMEM],
        out_specs=VMEM,
        out_shape=jax.ShapeDtypeStruct(many.shape[1:], F32),
        compiler_params=params(4),
        cost_estimate=FREE,
    )(many)
    return [plane] + [rotate(plane, "z", 4, k) for k in (1, 2, 3)]


def grad_kernel(width, place, s0, s1, s2, s3, sl_ref, tl_ref, ids, grad, column):
    for k, got in enumerate((s0, s1, s2, s3)):
        column[(place[1] + 4 - k) % 4] = got[...]
    m = merged(column[...])
    top_s, top_t, total_s, total_t, weighted_s, weighted_t, pick_s, pick_t = (
        v.reshape(1, LANES) for v in m
    )
    norm_s = top_s + jnp.log(total_s)
    norm_t = top_t + jnp.log(total_t)
    divergence = FACTOR * (weighted_s / total_s - norm_s) - (weighted_t / total_s - norm_t)
    advantage = jnp.clip(pick_t - norm_t - (pick_s - norm_s), -ADVANTAGE_CLIP, ADVANTAGE_CLIP)
    loss = divergence - advantage * (pick_s - norm_s)
    sl, tl = sl_ref[...], tl_ref[...]
    row = lax.broadcasted_iota(jnp.int32, sl.shape, 0)
    onehot = row == ids[...] - place[0] * width
    probs = jnp.exp(sl - top_s) * (1.0 / total_s)
    inner = FACTOR * (sl - norm_s) - (tl - norm_t) - divergence
    out = probs * inner - advantage * (onehot.astype(F32) - probs)

    full = width // 16 * 16
    parts = []
    for _ in range(3):
        parts.append(loss.astype(BF16).astype(F32))
        loss = loss - parts[-1]
    blank = jnp.zeros((grad.shape[0] - width - 3, LANES), F32)
    grad[:full] = out[:full].astype(BF16)
    grad[full:] = jnp.concatenate([out[full:], *parts, blank], axis=0).astype(BF16)


def logit_grad(place, column, sl, tl, ids):
    width = sl.shape[0]
    rows = (width + 3 + 15) // 16 * 16
    return pl.pallas_call(
        functools.partial(grad_kernel, width),
        in_specs=[SMEM] + [VMEM] * 7,
        out_specs=VMEM,
        out_shape=jax.ShapeDtypeStruct((rows, LANES), BF16),
        scratch_shapes=[pltpu.VMEM((4, 8, LANES), F32)],
        compiler_params=params(16),
        cost_estimate=FREE,
    )(place, *column, sl, tl, ids)


def hidden_kernel(place, *refs):
    grads, w, out = refs[:-2], refs[-2], refs[-1]
    width, depth = w.shape
    for n, g in enumerate(grads):
        part = lax.dot_general(
            g[:width], w[...], (((0,), (0,)), ((), ())), preferred_element_type=F32
        )
        first = 8 * (place[2] ^ (n % 2))
        rows = pl.ds(16 * (n // 2), 16)
        out[pl.ds(first, 8), rows] = part.reshape(8, 16, depth).astype(BF16)


def hidden_part(place, pairs, w, flops):
    depth, n = w.shape[1], len(pairs)
    return pl.pallas_call(
        hidden_kernel,
        in_specs=[SMEM] + [VMEM] * (2 * n + 1),
        out_specs=VMEM,
        out_shape=jax.ShapeDtypeStruct((16, 16 * n, depth), BF16),
        compiler_params=params(24),
        cost_estimate=estimate(flops),
    )(place, *[v for pair in pairs for v in pair], w)


def scatter(part):
    return lax.all_to_all(part, ("y", "x"), 0, 0)


def summed(parts):
    got = jnp.sum(parts.astype(F32), axis=0)
    return got.reshape(-1, 16, got.shape[1])


def weight_kernel(loss_row, _, *refs):
    g = jnp.concatenate([r[...] for r in refs[:8]], axis=1)
    h = jnp.concatenate([r[...] for r in refs[8:16]], axis=0)
    refs[16][...] = jnp.dot(g, h, preferred_element_type=F32).astype(BF16)

    @pl.when(pl.program_id(0) == pl.num_programs(0) - 1)
    def _():
        first = loss_row // 16 * 16
        ends = [r[first : first + 16].astype(F32) for r in refs[:8]]
        at = loss_row - first
        v = [(e[at : at + 1] + e[at + 1 : at + 2]) + e[at + 2 : at + 3] for e in ends]
        near = (v[0] + v[1]) + (v[4] + v[5])
        far = (v[2] + v[3]) + (v[6] + v[7])
        refs[17][...] = jnp.broadcast_to(near + far, refs[17].shape)


def weight_grad(width, grads, hidden, blocks):
    depth = hidden.shape[1]
    block = 256
    loss_row = width % block
    assert loss_row + 3 <= block

    def rows(d):
        return pl.BlockSpec((block, d), lambda i, sc: (i, 0))

    def owned(k):
        return pl.BlockSpec((LANES, depth), lambda i, sc: (sc[k], 0))

    return pl.pallas_call(
        functools.partial(weight_kernel, loss_row),
        grid_spec=pltpu.PrefetchScalarGridSpec(
            num_scalar_prefetch=1,
            grid=(pl.cdiv(width, block),),
            in_specs=[rows(LANES)] * 8 + [owned(k) for k in range(8)],
            out_specs=[rows(depth), pl.BlockSpec((8, LANES), lambda i, sc: (0, 0))],
        ),
        out_shape=[
            jax.ShapeDtypeStruct((width, depth), BF16),
            jax.ShapeDtypeStruct((8, LANES), F32),
        ],
        compiler_params=params(24),
        cost_estimate=pl.CostEstimate(
            flops=16 * LANES * width * depth, bytes_accessed=4 * width * depth, transcendentals=0
        ),
    )(blocks, *grads, *([hidden] * 8))


def shards(teacher_hidden, teacher_weight, student_hidden, student_weight, rollout_ids):
    g, s, z = lax.axis_index("g"), lax.axis_index("s"), lax.axis_index("z")
    index = (z * 4 + lax.axis_index("y")) * 4 + lax.axis_index("x")
    place = jnp.stack([index, z, s]).astype(jnp.int32)
    tokens, depth = student_hidden.shape
    wt, ws = teacher_weight.T, student_weight.T
    width = ws.shape[0]

    def block_of(c, gr, sr):
        return 4 * (g ^ gr) + 2 * c + (s ^ sr)

    blocks = jnp.stack(
        [block_of(c, gr, sr) for c in range(2) for gr in range(2) for sr in range(2)]
    ).astype(jnp.int32)

    def core_sums(grp, core):
        give_s = swap(partial_logits(ws, student_hidden, grp, 1 - core), "s")
        give_t = swap(partial_logits(wt, teacher_hidden, grp, 1 - core), "s")
        keep_s = partial_logits(ws, student_hidden, grp, core)
        keep_t = partial_logits(wt, teacher_hidden, grp, core)
        return (keep_s, give_s), (keep_t, give_t)

    here = rollout_ids.reshape(2, LANES)
    other = swap(lax.dynamic_index_in_dim(here, 1 - s, 0, keepdims=True), "s")
    mine = lax.dynamic_index_in_dim(here, s, 0, keepdims=True)
    ids = [jnp.where(s == c, mine, other) for c in range(2)]

    codes0, codes1 = encode(*core_sums(1 - g, s))
    far0 = swap(codes0, "g")
    near_blocks = jnp.stack([block_of(c, 0, sr) for sr in range(2) for c in range(2)])
    keep_s, give_s, keep_t, give_t = near_logits(
        ordered(near_blocks.astype(jnp.int32), codes0), student_hidden, teacher_hidden, ws, wt
    )
    near = (keep_s, swap(give_s, "s")), (keep_t, swap(give_t, "s"))
    far1 = swap(ordered(codes1, far0), "g")
    sl0, tl0, stats0 = local_stats(place, 0, *near, far0, (HIDES, 1), ids[0])
    grad0 = logit_grad(place, all_stats(stats0), sl0, tl0, ids[0])
    away0 = swap(grad0, "g")
    sl1, tl1, stats1 = local_stats(place, 1, *near, far1, (1, SECOND), ordered(ids[1], grad0))
    grad1 = logit_grad(place, all_stats(stats1), sl1, tl1, ids[1])
    away1 = swap(ordered(grad1, away0), "g")
    after = (grad0, ordered(away0, grad1), grad1, away1)
    pairs = [(v, swap(v, "s")) for v in after]
    early = scatter(hidden_part(place, pairs[:2], ws, 1))
    part = hidden_part(place, pairs[2:], ws, LAST)
    late = scatter(ordered(part, early))
    grads = [v for pair in pairs for v in pair]
    grad_weight, losses = weight_grad(width, grads, student_hidden, ordered(blocks, part))
    late = ordered(late, losses)
    sums = jnp.concatenate([summed(early), summed(late)], axis=0)

    def block(dest):
        return lax.dynamic_index_in_dim(
            sums, 2 * (dest % 2) + (g ^ (dest // 2)), 0, keepdims=False
        )

    total = block(z)
    for k in (1, 2, 3):
        total = total + rotate(block((z + k) % 4), "z", 4, k)
    return total.astype(BF16), grad_weight.T, jnp.sum(losses[0]) / tokens


def solution(mesh):
    split = Mesh(mesh.devices.reshape(2, 2, 4, 4, 4), ("g", "s", "z", "y", "x"))
    owners, vocab = ("g", "s"), ("z", "y", "x")
    return jax.shard_map(
        shards,
        mesh=split,
        in_specs=(P(None, owners), P(owners, vocab), P(None, owners), P(owners, vocab), P(owners)),
        out_specs=(P(vocab, owners), P(owners, vocab), P()),
        check_vma=False,
    )
```

```python
import functools

import jax
import jax.numpy as jnp
from jax import lax
from jax.experimental import pallas as pl
from jax.experimental.pallas import tpu as pltpu
from jax.sharding import Mesh
from jax.sharding import PartitionSpec as P

ENTROPY_WEIGHT = 0.1
FACTOR = 1.0 + ENTROPY_WEIGHT
ADVANTAGE_CLIP = 2.0
LANES = 128
LEVELS = 32700.0
HIDES = 30_000_000_000
LAST = 8_200_000_000
SECOND = HIDES // 8
VMEM = pl.BlockSpec(memory_space=pltpu.VMEM)
SMEM = pl.BlockSpec(memory_space=pltpu.SMEM)
F32, BF16 = jnp.float32, jnp.bfloat16


def estimate(flops):
    return pl.CostEstimate(flops=flops, bytes_accessed=1, transcendentals=0)


FREE = estimate(1)


def params(mib):
    return pltpu.CompilerParams(vmem_limit_bytes=mib * 2**20)


def swap(x, axis):
    return lax.ppermute(x, axis, [(0, 1), (1, 0)])


def rotate(x, axis, size, step):
    return lax.ppermute(x, axis, [(i, (i + step) % size) for i in range(size)])


def ordered(x, *earlier):
    return lax.optimization_barrier((x, *earlier))[0]


def partial_logits(weight, hidden, grp, core):
    parts = hidden.reshape(2, 2, 2, LANES, hidden.shape[1])
    rows = lax.dynamic_slice(parts, (grp, 0, core, 0, 0), (1, 2, 1, *parts.shape[3:]))
    rows = rows.reshape(2 * LANES, hidden.shape[1])
    return lax.dot_general(weight, rows, (((1,), (1,)), ((), ())), preferred_element_type=F32)


def near_kernel(width, _, *refs):
    hs, ht, ws, wt, outs, rs, rt = refs[:4], refs[4:8], refs[8], refs[9], refs[10:14], refs[14], refs[15]
    step = pl.program_id(0)

    @pl.when(step == 0)
    def _():
        for k in range(4):
            rs[LANES * k : LANES * (k + 1)] = hs[k][...]
            rt[LANES * k : LANES * (k + 1)] = ht[k][...]

    for head, (w, r) in enumerate(((ws, rs), (wt, rt))):
        out = lax.dot_general(w[...], r[...], (((1,), (1,)), ((), ())), preferred_element_type=F32)
        outs[2 * head][...] = out[:, : 2 * LANES]
        outs[2 * head + 1][...] = out[:, 2 * LANES :]


def near_logits(blocks, hidden_s, hidden_t, ws, wt):
    width = ws.shape[0]
    ds, dt = hidden_s.shape[1], hidden_t.shape[1]
    tile = 2 * LANES

    def rows(k, d):
        return pl.BlockSpec((LANES, d), lambda i, sc: (sc[k], 0))

    def part(d):
        return pl.BlockSpec((tile, d), lambda i, sc: (i, 0))

    return pl.pallas_call(
        functools.partial(near_kernel, width),
        grid_spec=pltpu.PrefetchScalarGridSpec(
            num_scalar_prefetch=1,
            grid=(pl.cdiv(width, tile),),
            in_specs=[rows(k, d) for d in (ds, dt) for k in range(4)] + [part(ds), part(dt)],
            out_specs=[part(2 * LANES)] * 4,
            scratch_shapes=[pltpu.VMEM((4 * LANES, ds), BF16), pltpu.VMEM((4 * LANES, dt), BF16)],
        ),
        out_shape=[jax.ShapeDtypeStruct((width, 2 * LANES), F32)] * 4,
        compiler_params=params(24),
        cost_estimate=FREE,
    )(blocks, *([hidden_s] * 4), *([hidden_t] * 4), ws, wt)


def code_kernel(width, as_, bs, at, bt, out):
    def put(v):
        return v.astype(jnp.int32).astype(jnp.int16)

    full = width // 16 * 16
    blank = jnp.zeros((out.shape[1] - width - 1, LANES), F32)
    for head, (a, b) in enumerate(((as_, bs), (at, bt))):
        x = a[...] + b[...]
        peak = jnp.max(jnp.abs(x), axis=0, keepdims=True)
        power = jnp.ceil(jnp.log2(jnp.maximum(peak, 1e-30) / LEVELS) * 256.0)
        scale = 1.0 / jnp.exp2(power * (1.0 / 256.0))
        code = jnp.clip(jnp.round(x * scale), -32767.0, 32767.0)
        out[head, :full] = put(code[:full])
        out[head, full:] = put(jnp.concatenate([code[full:], power, blank], axis=0))


def encode(c, student, teacher):
    width = student[0].shape[0]
    rows = (width + 1 + 15) // 16 * 16
    return pl.pallas_call(
        functools.partial(code_kernel, width),
        grid=(1,),
        in_specs=[pl.BlockSpec((width, LANES), lambda i: (0, c))] * 4,
        out_specs=pl.BlockSpec((2, rows, LANES), lambda i: (0, 0, 0)),
        out_shape=jax.ShapeDtypeStruct((2, rows, LANES), jnp.int16),
        compiler_params=params(16),
        cost_estimate=FREE,
    )(*student, *teacher)


def units_kernel(width, codes, units):
    full = width // 16 * 16
    for head in range(2):
        end = codes[head, full:].astype(jnp.int32).astype(F32)
        power = end[width - full : width - full + 1]
        units[head] = jnp.broadcast_to(jnp.exp2(power * (1.0 / 256.0)), (8, LANES))


def code_units(width, codes, flops):
    rows = codes.shape[1] - width // 16 * 16
    block = pl.BlockSpec(codes.shape, lambda: (0, 0, 0))
    return pl.pallas_call(
        functools.partial(units_kernel, width),
        in_specs=[block],
        out_specs=VMEM,
        out_shape=jax.ShapeDtypeStruct((2, 8, LANES), F32),
        compiler_params=params(8),
        cost_estimate=estimate(flops),
    )(codes)


def stats_kernel(width, place, as_, bs, at, bt, codes, units, ids, sl_ref, tl_ref, stats):
    def decoded(head):
        return codes[head].astype(jnp.int32).astype(F32)[:width] * units[head, :1]

    sl = as_[...] + bs[...] + decoded(0)
    tl = at[...] + bt[...] + decoded(1)
    sl_ref[...] = sl
    tl_ref[...] = tl
    own_s = jnp.max(sl, axis=0, keepdims=True)
    own_t = jnp.max(tl, axis=0, keepdims=True)
    es = jnp.exp(sl - own_s)
    row = lax.broadcasted_iota(jnp.int32, sl.shape, 0)
    onehot = row == ids[...] - place[0] * width

    def total(x):
        return jnp.sum(x, axis=0, keepdims=True)

    rows = [
        own_s,
        own_t,
        total(es),
        total(jnp.exp(tl - own_t)),
        total(es * sl),
        total(es * tl),
        total(jnp.where(onehot, sl, 0.0)),
        total(jnp.where(onehot, tl, 0.0)),
    ]
    stats[...] = jnp.broadcast_to(jnp.concatenate(rows, axis=0)[None], stats.shape)


def local_stats(place, c, student, teacher, codes, flops, ids):
    width = student[0].shape[0]
    size = width * LANES
    half = pl.BlockSpec((width, LANES), lambda i: (0, c))

    def whole(*shape):
        return pl.BlockSpec(shape, lambda i: (0,) * len(shape))

    return pl.pallas_call(
        functools.partial(stats_kernel, width),
        grid=(1,),
        in_specs=[SMEM] + [half] * 4 + [whole(*codes.shape), whole(2, 8, LANES), whole(1, LANES)],
        out_specs=[whole(width, LANES)] * 2 + [whole(16, 8, LANES)],
        out_shape=[jax.ShapeDtypeStruct((width, LANES), F32)] * 2
        + [jax.ShapeDtypeStruct((16, 8, LANES), F32)],
        compiler_params=params(24),
        cost_estimate=estimate(flops[1]),
    )(place, *student, *teacher, codes, code_units(width, codes, flops[0]), ids)


def merged(many):
    top_s, top_t = jnp.max(many[:, 0], axis=0), jnp.max(many[:, 1], axis=0)
    fs, ft = jnp.exp(many[:, 0] - top_s), jnp.exp(many[:, 1] - top_t)
    return [
        top_s,
        top_t,
        jnp.sum(many[:, 2] * fs, axis=0),
        jnp.sum(many[:, 3] * ft, axis=0),
        jnp.sum(many[:, 4] * fs, axis=0),
        jnp.sum(many[:, 5] * fs, axis=0),
        jnp.sum(many[:, 6], axis=0),
        jnp.sum(many[:, 7], axis=0),
    ]


def merge_kernel(many, out):
    out[...] = jnp.stack(merged(many[...]))


def all_stats(stats):
    many = lax.all_to_all(stats, ("y", "x"), 0, 0)
    plane = pl.pallas_call(
        merge_kernel,
        in_specs=[VMEM],
        out_specs=VMEM,
        out_shape=jax.ShapeDtypeStruct(many.shape[1:], F32),
        compiler_params=params(4),
        cost_estimate=FREE,
    )(many)
    return [plane] + [rotate(plane, "z", 4, k) for k in (1, 2, 3)]


def grad_kernel(width, place, s0, s1, s2, s3, sl_ref, tl_ref, ids, grad, column):
    for k, got in enumerate((s0, s1, s2, s3)):
        column[(place[1] + 4 - k) % 4] = got[...]
    m = merged(column[...])
    top_s, top_t, total_s, total_t, weighted_s, weighted_t, pick_s, pick_t = (
        v.reshape(1, LANES) for v in m
    )
    norm_s = top_s + jnp.log(total_s)
    norm_t = top_t + jnp.log(total_t)
    divergence = FACTOR * (weighted_s / total_s - norm_s) - (weighted_t / total_s - norm_t)
    advantage = jnp.clip(pick_t - norm_t - (pick_s - norm_s), -ADVANTAGE_CLIP, ADVANTAGE_CLIP)
    loss = divergence - advantage * (pick_s - norm_s)
    sl, tl = sl_ref[...], tl_ref[...]
    row = lax.broadcasted_iota(jnp.int32, sl.shape, 0)
    onehot = row == ids[...] - place[0] * width
    probs = jnp.exp(sl - top_s) * (1.0 / total_s)
    inner = FACTOR * (sl - norm_s) - (tl - norm_t) - divergence
    out = probs * inner - advantage * (onehot.astype(F32) - probs)

    full = width // 16 * 16
    parts = []
    for _ in range(3):
        parts.append(loss.astype(BF16).astype(F32))
        loss = loss - parts[-1]
    blank = jnp.zeros((grad.shape[0] - width - 3, LANES), F32)
    grad[:full] = out[:full].astype(BF16)
    grad[full:] = jnp.concatenate([out[full:], *parts, blank], axis=0).astype(BF16)


def logit_grad(place, column, sl, tl, ids):
    width = sl.shape[0]
    rows = (width + 3 + 15) // 16 * 16
    return pl.pallas_call(
        functools.partial(grad_kernel, width),
        in_specs=[SMEM] + [VMEM] * 7,
        out_specs=VMEM,
        out_shape=jax.ShapeDtypeStruct((rows, LANES), BF16),
        scratch_shapes=[pltpu.VMEM((4, 8, LANES), F32)],
        compiler_params=params(16),
        cost_estimate=FREE,
    )(place, *column, sl, tl, ids)


def hidden_kernel(place, *refs):
    grads, w, out = refs[:-2], refs[-2], refs[-1]
    width, depth = w.shape
    for n, g in enumerate(grads):
        part = lax.dot_general(
            g[:width], w[...], (((0,), (0,)), ((), ())), preferred_element_type=F32
        )
        first = 8 * (place[2] ^ (n % 2))
        rows = pl.ds(16 * (n // 2), 16)
        out[pl.ds(first, 8), rows] = part.reshape(8, 16, depth).astype(BF16)


def hidden_part(place, pairs, w, flops):
    depth, n = w.shape[1], len(pairs)
    return pl.pallas_call(
        hidden_kernel,
        in_specs=[SMEM] + [VMEM] * (2 * n + 1),
        out_specs=VMEM,
        out_shape=jax.ShapeDtypeStruct((16, 16 * n, depth), BF16),
        compiler_params=params(24),
        cost_estimate=estimate(flops),
    )(place, *[v for pair in pairs for v in pair], w)


def scatter(part):
    return lax.all_to_all(part, ("y", "x"), 0, 0)


def summed(parts):
    got = jnp.sum(parts.astype(F32), axis=0)
    return got.reshape(-1, 16, got.shape[1])


def weight_kernel(loss_row, _, *refs):
    g = jnp.concatenate([r[...] for r in refs[:8]], axis=1)
    h = jnp.concatenate([r[...] for r in refs[8:16]], axis=0)
    refs[16][...] = jnp.dot(g, h, preferred_element_type=F32).astype(BF16)

    @pl.when(pl.program_id(0) == pl.num_programs(0) - 1)
    def _():
        first = loss_row // 16 * 16
        ends = [r[first : first + 16].astype(F32) for r in refs[:8]]
        at = loss_row - first
        v = [(e[at : at + 1] + e[at + 1 : at + 2]) + e[at + 2 : at + 3] for e in ends]
        near = (v[0] + v[1]) + (v[4] + v[5])
        far = (v[2] + v[3]) + (v[6] + v[7])
        refs[17][...] = jnp.broadcast_to(near + far, refs[17].shape)


def weight_grad(width, grads, hidden, blocks):
    depth = hidden.shape[1]
    block = 256
    loss_row = width % block
    assert loss_row + 3 <= block

    def rows(d):
        return pl.BlockSpec((block, d), lambda i, sc: (i, 0))

    def owned(k):
        return pl.BlockSpec((LANES, depth), lambda i, sc: (sc[k], 0))

    return pl.pallas_call(
        functools.partial(weight_kernel, loss_row),
        grid_spec=pltpu.PrefetchScalarGridSpec(
            num_scalar_prefetch=1,
            grid=(pl.cdiv(width, block),),
            in_specs=[rows(LANES)] * 8 + [owned(k) for k in range(8)],
            out_specs=[rows(depth), pl.BlockSpec((8, LANES), lambda i, sc: (0, 0))],
        ),
        out_shape=[
            jax.ShapeDtypeStruct((width, depth), BF16),
            jax.ShapeDtypeStruct((8, LANES), F32),
        ],
        compiler_params=params(24),
        cost_estimate=pl.CostEstimate(
            flops=16 * LANES * width * depth, bytes_accessed=4 * width * depth, transcendentals=0
        ),
    )(blocks, *grads, *([hidden] * 8))


def shards(teacher_hidden, teacher_weight, student_hidden, student_weight, rollout_ids):
    g, s, z = lax.axis_index("g"), lax.axis_index("s"), lax.axis_index("z")
    index = (z * 4 + lax.axis_index("y")) * 4 + lax.axis_index("x")
    place = jnp.stack([index, z, s]).astype(jnp.int32)
    tokens, depth = student_hidden.shape
    wt, ws = teacher_weight.T, student_weight.T
    width = ws.shape[0]

    def block_of(c, gr, sr):
        return 4 * (g ^ gr) + 2 * c + (s ^ sr)

    blocks = jnp.stack(
        [block_of(c, gr, sr) for c in range(2) for gr in range(2) for sr in range(2)]
    ).astype(jnp.int32)

    def core_sums(grp, core):
        give_s = swap(partial_logits(ws, student_hidden, grp, 1 - core), "s")
        give_t = swap(partial_logits(wt, teacher_hidden, grp, 1 - core), "s")
        keep_s = partial_logits(ws, student_hidden, grp, core)
        keep_t = partial_logits(wt, teacher_hidden, grp, core)
        return (keep_s, give_s), (keep_t, give_t)

    here = rollout_ids.reshape(2, LANES)
    other = swap(lax.dynamic_index_in_dim(here, 1 - s, 0, keepdims=True), "s")
    mine = lax.dynamic_index_in_dim(here, s, 0, keepdims=True)
    ids = [jnp.where(s == c, mine, other) for c in range(2)]

    far_sums = core_sums(1 - g, s)
    codes0 = encode(0, *far_sums)
    far0 = swap(codes0, "g")
    codes1 = encode(1, *far_sums)
    near_blocks = jnp.stack([block_of(c, 0, sr) for sr in range(2) for c in range(2)])
    keep_s, give_s, keep_t, give_t = near_logits(
        ordered(near_blocks.astype(jnp.int32), codes0, codes1), student_hidden, teacher_hidden, ws, wt
    )
    near = (keep_s, swap(give_s, "s")), (keep_t, swap(give_t, "s"))
    far1 = swap(ordered(codes1, far0), "g")
    sl0, tl0, stats0 = local_stats(place, 0, *near, far0, (HIDES, 1), ids[0])
    grad0 = logit_grad(place, all_stats(stats0), sl0, tl0, ids[0])
    away0 = swap(grad0, "g")
    sl1, tl1, stats1 = local_stats(place, 1, *near, far1, (1, SECOND), ordered(ids[1], grad0))
    grad1 = logit_grad(place, all_stats(stats1), sl1, tl1, ids[1])
    away1 = swap(ordered(grad1, away0), "g")
    after = (grad0, ordered(away0, grad1), grad1, away1)
    pairs = [(v, swap(v, "s")) for v in after]
    early = scatter(hidden_part(place, pairs[:2], ws, 1))
    part = hidden_part(place, pairs[2:], ws, LAST)
    late = scatter(ordered(part, early))
    grads = [v for pair in pairs for v in pair]
    grad_weight, losses = weight_grad(width, grads, student_hidden, ordered(blocks, part))
    late = ordered(late, losses)
    sums = jnp.concatenate([summed(early), summed(late)], axis=0)

    def block(dest):
        return lax.dynamic_index_in_dim(
            sums, 2 * (dest % 2) + (g ^ (dest // 2)), 0, keepdims=False
        )

    total = block(z)
    for k in (1, 2, 3):
        total = total + rotate(block((z + k) % 4), "z", 4, k)
    return total.astype(BF16), grad_weight.T, jnp.sum(losses[0]) / tokens


def solution(mesh):
    split = Mesh(mesh.devices.reshape(2, 2, 4, 4, 4), ("g", "s", "z", "y", "x"))
    owners, vocab = ("g", "s"), ("z", "y", "x")
    return jax.shard_map(
        shards,
        mesh=split,
        in_specs=(P(None, owners), P(owners, vocab), P(None, owners), P(owners, vocab), P(owners)),
        out_specs=(P(vocab, owners), P(owners, vocab), P()),
        check_vma=False,
    )
```

```python
import functools

import jax
import jax.numpy as jnp
from jax import lax
from jax.experimental import pallas as pl
from jax.experimental.pallas import tpu as pltpu
from jax.sharding import Mesh
from jax.sharding import PartitionSpec as P

ENTROPY_WEIGHT = 0.1
FACTOR = 1.0 + ENTROPY_WEIGHT
ADVANTAGE_CLIP = 2.0
LANES = 128
LEVELS = 32700.0
HIDES = 30_000_000_000
LAST = 8_200_000_000
SECOND = HIDES // 8
VMEM = pl.BlockSpec(memory_space=pltpu.VMEM)
SMEM = pl.BlockSpec(memory_space=pltpu.SMEM)
F32, BF16 = jnp.float32, jnp.bfloat16


def estimate(flops):
    return pl.CostEstimate(flops=flops, bytes_accessed=1, transcendentals=0)


FREE = estimate(1)


def params(mib):
    return pltpu.CompilerParams(vmem_limit_bytes=mib * 2**20)


def swap(x, axis):
    return lax.ppermute(x, axis, [(0, 1), (1, 0)])


def rotate(x, axis, size, step):
    return lax.ppermute(x, axis, [(i, (i + step) % size) for i in range(size)])


def ordered(x, *earlier):
    return lax.optimization_barrier((x, *earlier))[0]


def partial_logits(weight, hidden, grp, core):
    parts = hidden.reshape(2, 2, 2, LANES, hidden.shape[1])
    rows = lax.dynamic_slice(parts, (grp, 0, core, 0, 0), (1, 2, 1, *parts.shape[3:]))
    rows = rows.reshape(2 * LANES, hidden.shape[1])
    return lax.dot_general(weight, rows, (((1,), (1,)), ((), ())), preferred_element_type=F32)


def near_kernel(width, _, *refs):
    hs, ht, ws, wt, outs, rs, rt = refs[:4], refs[4:8], refs[8], refs[9], refs[10:14], refs[14], refs[15]
    step = pl.program_id(0)

    @pl.when(step == 0)
    def _():
        for k in range(4):
            rs[LANES * k : LANES * (k + 1)] = hs[k][...]
            rt[LANES * k : LANES * (k + 1)] = ht[k][...]

    for head, (w, r) in enumerate(((ws, rs), (wt, rt))):
        out = lax.dot_general(w[...], r[...], (((1,), (1,)), ((), ())), preferred_element_type=F32)
        outs[2 * head][...] = out[:, : 2 * LANES]
        outs[2 * head + 1][...] = out[:, 2 * LANES :]


def near_logits(blocks, hidden_s, hidden_t, ws, wt):
    width = ws.shape[0]
    ds, dt = hidden_s.shape[1], hidden_t.shape[1]
    tile = 2 * LANES

    def rows(k, d):
        return pl.BlockSpec((LANES, d), lambda i, sc: (sc[k], 0))

    def part(d):
        return pl.BlockSpec((tile, d), lambda i, sc: (i, 0))

    return pl.pallas_call(
        functools.partial(near_kernel, width),
        grid_spec=pltpu.PrefetchScalarGridSpec(
            num_scalar_prefetch=1,
            grid=(pl.cdiv(width, tile),),
            in_specs=[rows(k, d) for d in (ds, dt) for k in range(4)] + [part(ds), part(dt)],
            out_specs=[part(2 * LANES)] * 4,
            scratch_shapes=[pltpu.VMEM((4 * LANES, ds), BF16), pltpu.VMEM((4 * LANES, dt), BF16)],
        ),
        out_shape=[jax.ShapeDtypeStruct((width, 2 * LANES), F32)] * 4,
        compiler_params=params(24),
        cost_estimate=FREE,
    )(blocks, *([hidden_s] * 4), *([hidden_t] * 4), ws, wt)


def code_kernel(width, as_, bs, at, bt, out):
    def put(v):
        return v.astype(jnp.int32).astype(jnp.int16)

    full = width // 16 * 16
    blank = jnp.zeros((out.shape[1] - width - 1, LANES), F32)
    for head, (a, b) in enumerate(((as_, bs), (at, bt))):
        x = a[...] + b[...]
        peak = jnp.max(jnp.abs(x), axis=0, keepdims=True)
        power = jnp.ceil(jnp.log2(jnp.maximum(peak, 1e-30) / LEVELS) * 256.0)
        scale = 1.0 / jnp.exp2(power * (1.0 / 256.0))
        code = jnp.clip(jnp.round(x * scale), -32767.0, 32767.0)
        out[head, :full] = put(code[:full])
        out[head, full:] = put(jnp.concatenate([code[full:], power, blank], axis=0))


def encode(c, student, teacher):
    width = student[0].shape[0]
    rows = (width + 1 + 15) // 16 * 16
    return pl.pallas_call(
        functools.partial(code_kernel, width),
        grid=(1,),
        in_specs=[pl.BlockSpec((width, LANES), lambda i: (0, c))] * 4,
        out_specs=pl.BlockSpec((2, rows, LANES), lambda i: (0, 0, 0)),
        out_shape=jax.ShapeDtypeStruct((2, rows, LANES), jnp.int16),
        compiler_params=params(16),
        cost_estimate=FREE,
    )(*student, *teacher)


def units_kernel(width, codes, units):
    full = width // 16 * 16
    for head in range(2):
        end = codes[head, full:].astype(jnp.int32).astype(F32)
        power = end[width - full : width - full + 1]
        units[head] = jnp.broadcast_to(jnp.exp2(power * (1.0 / 256.0)), (8, LANES))


def code_units(width, codes, flops):
    rows = codes.shape[1] - width // 16 * 16
    block = pl.BlockSpec(codes.shape, lambda: (0, 0, 0))
    return pl.pallas_call(
        functools.partial(units_kernel, width),
        in_specs=[block],
        out_specs=VMEM,
        out_shape=jax.ShapeDtypeStruct((2, 8, LANES), F32),
        compiler_params=params(8),
        cost_estimate=estimate(flops),
    )(codes)


def stats_kernel(width, place, as_, bs, at, bt, codes, units, ids, sl_ref, tl_ref, stats):
    def decoded(head):
        return codes[head].astype(jnp.int32).astype(F32)[:width] * units[head, :1]

    sl = as_[...] + bs[...] + decoded(0)
    tl = at[...] + bt[...] + decoded(1)
    sl_ref[...] = sl
    tl_ref[...] = tl
    own_s = jnp.max(sl, axis=0, keepdims=True)
    own_t = jnp.max(tl, axis=0, keepdims=True)
    es = jnp.exp(sl - own_s)
    row = lax.broadcasted_iota(jnp.int32, sl.shape, 0)
    onehot = row == ids[...] - place[0] * width

    def total(x):
        return jnp.sum(x, axis=0, keepdims=True)

    rows = [
        own_s,
        own_t,
        total(es),
        total(jnp.exp(tl - own_t)),
        total(es * sl),
        total(es * tl),
        total(jnp.where(onehot, sl, 0.0)),
        total(jnp.where(onehot, tl, 0.0)),
    ]
    stats[...] = jnp.broadcast_to(jnp.concatenate(rows, axis=0)[None], stats.shape)


def local_stats(place, c, student, teacher, codes, flops, ids):
    width = student[0].shape[0]
    size = width * LANES
    half = pl.BlockSpec((width, LANES), lambda i: (0, c))

    def whole(*shape):
        return pl.BlockSpec(shape, lambda i: (0,) * len(shape))

    return pl.pallas_call(
        functools.partial(stats_kernel, width),
        grid=(1,),
        in_specs=[SMEM] + [half] * 4 + [whole(*codes.shape), whole(2, 8, LANES), whole(1, LANES)],
        out_specs=[whole(width, LANES)] * 2 + [whole(16, 8, LANES)],
        out_shape=[jax.ShapeDtypeStruct((width, LANES), F32)] * 2
        + [jax.ShapeDtypeStruct((16, 8, LANES), F32)],
        compiler_params=params(24),
        cost_estimate=estimate(flops[1]),
    )(place, *student, *teacher, codes, code_units(width, codes, flops[0]), ids)


def merged(many):
    top_s, top_t = jnp.max(many[:, 0], axis=0), jnp.max(many[:, 1], axis=0)
    fs, ft = jnp.exp(many[:, 0] - top_s), jnp.exp(many[:, 1] - top_t)
    return [
        top_s,
        top_t,
        jnp.sum(many[:, 2] * fs, axis=0),
        jnp.sum(many[:, 3] * ft, axis=0),
        jnp.sum(many[:, 4] * fs, axis=0),
        jnp.sum(many[:, 5] * fs, axis=0),
        jnp.sum(many[:, 6], axis=0),
        jnp.sum(many[:, 7], axis=0),
    ]


def merge_kernel(many, out):
    out[...] = jnp.stack(merged(many[...]))


def all_stats(stats):
    many = lax.all_to_all(stats, ("y", "x"), 0, 0)
    plane = pl.pallas_call(
        merge_kernel,
        in_specs=[VMEM],
        out_specs=VMEM,
        out_shape=jax.ShapeDtypeStruct(many.shape[1:], F32),
        compiler_params=params(4),
        cost_estimate=FREE,
    )(many)
    return [plane] + [rotate(plane, "z", 4, k) for k in (1, 2, 3)]


def grad_kernel(width, place, s0, s1, s2, s3, sl_ref, tl_ref, ids, grad, column):
    for k, got in enumerate((s0, s1, s2, s3)):
        column[(place[1] + 4 - k) % 4] = got[...]
    m = merged(column[...])
    top_s, top_t, total_s, total_t, weighted_s, weighted_t, pick_s, pick_t = (
        v.reshape(1, LANES) for v in m
    )
    norm_s = top_s + jnp.log(total_s)
    norm_t = top_t + jnp.log(total_t)
    divergence = FACTOR * (weighted_s / total_s - norm_s) - (weighted_t / total_s - norm_t)
    advantage = jnp.clip(pick_t - norm_t - (pick_s - norm_s), -ADVANTAGE_CLIP, ADVANTAGE_CLIP)
    loss = divergence - advantage * (pick_s - norm_s)
    sl, tl = sl_ref[...], tl_ref[...]
    row = lax.broadcasted_iota(jnp.int32, sl.shape, 0)
    onehot = row == ids[...] - place[0] * width
    probs = jnp.exp(sl - top_s) * (1.0 / total_s)
    inner = FACTOR * (sl - norm_s) - (tl - norm_t) - divergence
    out = probs * inner - advantage * (onehot.astype(F32) - probs)

    full = width // 16 * 16
    parts = []
    for _ in range(3):
        parts.append(loss.astype(BF16).astype(F32))
        loss = loss - parts[-1]
    blank = jnp.zeros((grad.shape[0] - width - 3, LANES), F32)
    grad[:full] = out[:full].astype(BF16)
    grad[full:] = jnp.concatenate([out[full:], *parts, blank], axis=0).astype(BF16)


def logit_grad(place, column, sl, tl, ids):
    width = sl.shape[0]
    rows = (width + 3 + 15) // 16 * 16
    return pl.pallas_call(
        functools.partial(grad_kernel, width),
        in_specs=[SMEM] + [VMEM] * 7,
        out_specs=VMEM,
        out_shape=jax.ShapeDtypeStruct((rows, LANES), BF16),
        scratch_shapes=[pltpu.VMEM((4, 8, LANES), F32)],
        compiler_params=params(16),
        cost_estimate=FREE,
    )(place, *column, sl, tl, ids)


def hidden_kernel(place, *refs):
    grads, w, out = refs[:-2], refs[-2], refs[-1]
    width, depth = w.shape
    for n, g in enumerate(grads):
        part = lax.dot_general(
            g[:width], w[...], (((0,), (0,)), ((), ())), preferred_element_type=F32
        )
        first = 8 * (place[2] ^ (n % 2))
        rows = pl.ds(16 * (n // 2), 16)
        out[pl.ds(first, 8), rows] = part.reshape(8, 16, depth).astype(BF16)


def hidden_part(place, pairs, w, flops):
    (width, depth), n = w.shape, len(pairs)
    tile = depth // 2
    return pl.pallas_call(
        hidden_kernel,
        grid=(2,),
        in_specs=[SMEM]
        + [pl.BlockSpec(v.shape, lambda i: (0, 0)) for pair in pairs for v in pair]
        + [pl.BlockSpec((width, tile), lambda i: (0, i))],
        out_specs=pl.BlockSpec((16, 16 * n, tile), lambda i: (0, 0, i)),
        out_shape=jax.ShapeDtypeStruct((16, 16 * n, depth), BF16),
        compiler_params=params(60),
        cost_estimate=estimate(flops),
    )(place, *[v for pair in pairs for v in pair], w)


def scatter(part):
    return lax.all_to_all(part, ("y", "x"), 0, 0)


def summed(parts):
    got = jnp.sum(parts.astype(F32), axis=0)
    return got.reshape(-1, 16, got.shape[1])


def weight_kernel(loss_row, _, *refs):
    g = jnp.concatenate([r[...] for r in refs[:8]], axis=1)
    h = jnp.concatenate([r[...] for r in refs[8:16]], axis=0)
    refs[16][...] = jnp.dot(g, h, preferred_element_type=F32).astype(BF16)

    @pl.when(pl.program_id(0) == pl.num_programs(0) - 1)
    def _():
        first = loss_row // 16 * 16
        ends = [r[first : first + 16].astype(F32) for r in refs[:8]]
        at = loss_row - first
        v = [(e[at : at + 1] + e[at + 1 : at + 2]) + e[at + 2 : at + 3] for e in ends]
        near = (v[0] + v[1]) + (v[4] + v[5])
        far = (v[2] + v[3]) + (v[6] + v[7])
        refs[17][...] = jnp.broadcast_to(near + far, refs[17].shape)


def weight_grad(width, grads, hidden, blocks):
    depth = hidden.shape[1]
    block = 256
    loss_row = width % block
    assert loss_row + 3 <= block

    def rows(d):
        return pl.BlockSpec((block, d), lambda i, sc: (i, 0))

    def owned(k):
        return pl.BlockSpec((LANES, depth), lambda i, sc: (sc[k], 0))

    return pl.pallas_call(
        functools.partial(weight_kernel, loss_row),
        grid_spec=pltpu.PrefetchScalarGridSpec(
            num_scalar_prefetch=1,
            grid=(pl.cdiv(width, block),),
            in_specs=[rows(LANES)] * 8 + [owned(k) for k in range(8)],
            out_specs=[rows(depth), pl.BlockSpec((8, LANES), lambda i, sc: (0, 0))],
        ),
        out_shape=[
            jax.ShapeDtypeStruct((width, depth), BF16),
            jax.ShapeDtypeStruct((8, LANES), F32),
        ],
        compiler_params=params(24),
        cost_estimate=pl.CostEstimate(
            flops=16 * LANES * width * depth, bytes_accessed=4 * width * depth, transcendentals=0
        ),
    )(blocks, *grads, *([hidden] * 8))


def shards(teacher_hidden, teacher_weight, student_hidden, student_weight, rollout_ids):
    g, s, z = lax.axis_index("g"), lax.axis_index("s"), lax.axis_index("z")
    index = (z * 4 + lax.axis_index("y")) * 4 + lax.axis_index("x")
    place = jnp.stack([index, z, s]).astype(jnp.int32)
    tokens, depth = student_hidden.shape
    wt, ws = teacher_weight.T, student_weight.T
    width = ws.shape[0]

    def block_of(c, gr, sr):
        return 4 * (g ^ gr) + 2 * c + (s ^ sr)

    blocks = jnp.stack(
        [block_of(c, gr, sr) for c in range(2) for gr in range(2) for sr in range(2)]
    ).astype(jnp.int32)

    def core_sums(grp, core):
        give_s = swap(partial_logits(ws, student_hidden, grp, 1 - core), "s")
        give_t = swap(partial_logits(wt, teacher_hidden, grp, 1 - core), "s")
        keep_s = partial_logits(ws, student_hidden, grp, core)
        keep_t = partial_logits(wt, teacher_hidden, grp, core)
        return (keep_s, give_s), (keep_t, give_t)

    here = rollout_ids.reshape(2, LANES)
    other = swap(lax.dynamic_index_in_dim(here, 1 - s, 0, keepdims=True), "s")
    mine = lax.dynamic_index_in_dim(here, s, 0, keepdims=True)
    ids = [jnp.where(s == c, mine, other) for c in range(2)]

    far_sums = core_sums(1 - g, s)
    codes0 = encode(0, *far_sums)
    far0 = swap(codes0, "g")
    codes1 = encode(1, *far_sums)
    near_blocks = jnp.stack([block_of(c, 0, sr) for sr in range(2) for c in range(2)])
    keep_s, give_s, keep_t, give_t = near_logits(
        ordered(near_blocks.astype(jnp.int32), codes0, codes1), student_hidden, teacher_hidden, ws, wt
    )
    near = (keep_s, swap(give_s, "s")), (keep_t, swap(give_t, "s"))
    far1 = swap(ordered(codes1, far0), "g")
    sl0, tl0, stats0 = local_stats(place, 0, *near, far0, (HIDES, 1), ids[0])
    grad0 = logit_grad(place, all_stats(stats0), sl0, tl0, ids[0])
    away0 = swap(grad0, "g")
    sl1, tl1, stats1 = local_stats(place, 1, *near, far1, (1, SECOND), ordered(ids[1], grad0))
    grad1 = logit_grad(place, all_stats(stats1), sl1, tl1, ids[1])
    away1 = swap(ordered(grad1, away0), "g")
    after = (grad0, ordered(away0, grad1), grad1, away1)
    pairs = [(v, swap(v, "s")) for v in after]
    early = scatter(hidden_part(place, pairs[:2], ws, 1))
    part = hidden_part(place, pairs[2:], ws, LAST)
    late = scatter(ordered(part, early))
    grads = [v for pair in pairs for v in pair]
    grad_weight, losses = weight_grad(width, grads, student_hidden, ordered(blocks, part))
    late = ordered(late, losses)
    sums = jnp.concatenate([summed(early), summed(late)], axis=0)

    def block(dest):
        return lax.dynamic_index_in_dim(
            sums, 2 * (dest % 2) + (g ^ (dest // 2)), 0, keepdims=False
        )

    total = block(z)
    for k in (1, 2, 3):
        total = total + rotate(block((z + k) % 4), "z", 4, k)
    return total.astype(BF16), grad_weight.T, jnp.sum(losses[0]) / tokens


def solution(mesh):
    split = Mesh(mesh.devices.reshape(2, 2, 4, 4, 4), ("g", "s", "z", "y", "x"))
    owners, vocab = ("g", "s"), ("z", "y", "x")
    return jax.shard_map(
        shards,
        mesh=split,
        in_specs=(P(None, owners), P(owners, vocab), P(None, owners), P(owners, vocab), P(owners)),
        out_specs=(P(vocab, owners), P(owners, vocab), P()),
        check_vma=False,
    )
```
